256 devices in a mesh: dp: 32 (over y, x, core), cent: 8 (over z).
Axes of the slice: x: 4, y: 4, z: 8, core: 2. Of those that a mesh axis runs over, the one named last changes fastest.
Arguments:
- emb: bfloat16 [524288, 768], P(('dp', 'cent')), may hold values from -37 to 37
- centroids: bfloat16 [8192, 768], P('cent'), may hold values from -4.1 to 4.1
- block_parent: int32 [4096], P(('dp', 'cent')), may hold values from 0 to 127, as said below
- block_live: int32 [4096], P(('dp', 'cent')), may hold values from 32 to 128
Outputs:
- new_centroids: float32 [8192, 768], P('cent')
The draws below stay inside these ranges and needn't reach their ends.
Inputs may be any that keep to these rules, and one draw needn't show every extreme that they name: Among the 16 blocks of one device (one index of dp+cent), at most 4 have parents owned by one index of cent (block_parent // 16), and exactly 4 for some index on every device.
All inputs are finite; a program needn't handle non-finite values.
Results may differ from the reference program's by a relative error of at most 0.0029.
Values may be sent and summed in bfloat16 or wider, within the bound.
No kernel may reach another device: no remote copies, remote signals or barrier semaphores. Data moves between devices by JAX's collectives and lax.ppermute only.
A program may use at most 128 MiB of HBM per device.

```python
import math
import jax
import jax.numpy as jnp
from jax import lax

D = 768
KIDS = 64
ROWBLK = 128
PAR_DEV = 16
BLK_DEV = 16
ITERS = 2
PRIOR = 64
PARENTS = 128
CENTS = 8192
BLOCKS = 4096
ROWS = 524288
N_CENT = 8


def parent_layout(key):
    key = jax.random.fold_in(key, 11)
    device_total = BLOCKS // BLK_DEV
    rank_of = jax.vmap(lambda device_no: jax.random.permutation(jax.random.fold_in(key, device_no), BLK_DEV))(jnp.arange(device_total))
    rank_of = rank_of.reshape(BLOCKS).astype(jnp.int32)
    group_of = jnp.arange(BLOCKS, dtype=jnp.int32) // BLK_DEV // N_CENT
    heavy_owner = jax.random.randint(jax.random.fold_in(key, 100003), (device_total // N_CENT,), 0, N_CENT)[group_of]
    capacity = BLK_DEV // 4
    spread = (heavy_owner + 1 + (rank_of - capacity) % (N_CENT - 1)) % N_CENT
    owner_idx = jnp.where(rank_of < capacity, heavy_owner, spread)
    within = jax.random.randint(jax.random.fold_in(key, 100007), (BLOCKS,), 0, PAR_DEV)
    return ((owner_idx * PAR_DEV + within).astype(jnp.int32), rank_of)


def centroid_table(key):
    base_draw = jnp.clip(jax.random.normal(jax.random.fold_in(key, 21), (PARENTS, KIDS, D), jnp.float32), -4.0, 4.0)
    second = base_draw[:, 1:2]
    return jnp.concatenate([base_draw[:, 0:1], second, base_draw[:, 2:]], axis=1)


def draw_centroids(key, part):
    kid_table = centroid_table(key)
    return kid_table.reshape(CENTS, D).astype(jnp.bfloat16)


def draw_block_parent(key, part):
    parents, rank_of = parent_layout(key)
    return parents


def draw_block_live(key, part):
    parents, rank_of = parent_layout(key)
    key = jax.random.fold_in(key, 2)
    short_by = jax.random.randint(key, (BLOCKS,), 0, 97)
    return jnp.where(rank_of == 0, ROWBLK, ROWBLK - short_by).astype(jnp.int32)


def draw_emb(key, part):
    closeness = 0.0
    kid_table = centroid_table(key)
    parents, rank_of = parent_layout(key)
    key = jax.random.fold_in(key, 3)
    noise_rows = jnp.clip(jax.random.normal(jax.random.fold_in(key, 1), (BLOCKS, ROWBLK, D), jnp.float32), -6.0, 6.0)
    row_label = jax.random.randint(jax.random.fold_in(key, 4), (BLOCKS, ROWBLK), 0, KIDS)
    drift = 3.0 * jnp.clip(jax.random.normal(jax.random.fold_in(key, 5), (PARENTS, KIDS, D), jnp.float32), -4.0, 4.0)
    targets = kid_table + drift
    centers = targets[parents[:, None], row_label]
    position = jnp.arange(ROWBLK, dtype=jnp.int32)
    aligned = closeness * (position % 32 == 0).astype(jnp.float32)
    spread_rows = noise_rows + 0.1 * centers
    drawn_rows = (1.0 - aligned)[None, :, None] * spread_rows
    return drawn_rows.reshape(ROWS, D).astype(jnp.bfloat16)


def setup_inputs(seed: int = 0) -> dict:
    arg_keys = jax.random.split(jax.random.key(seed), 5)
    return {
        "emb": draw_emb(jax.random.fold_in(arg_keys[4], 71), 0),
        "centroids": draw_centroids(jax.random.fold_in(arg_keys[4], 71), 0),
        "block_parent": draw_block_parent(jax.random.fold_in(arg_keys[4], 71), 0),
        "block_live": draw_block_live(jax.random.fold_in(arg_keys[4], 71), 0),
    }


softness = 0.8

def block_terms(members, children, live_rows):
    children32 = children.astype(jnp.float32)
    products = jnp.einsum('grd,gkd->grk', members.astype(jnp.float32), children32)
    squares = lax.optimization_barrier(jnp.sum(children32 * children32, axis=-1))
    logits = (2.0 * products - squares[:, None, :]) / (softness * math.sqrt(D))
    row_top = lax.optimization_barrier(jnp.max(logits, axis=-1, keepdims=True))
    scaled = jnp.exp(logits - row_top)
    weights = scaled / lax.optimization_barrier(jnp.sum(scaled, axis=-1, keepdims=True))
    inside = jnp.arange(members.shape[1], dtype=jnp.int32)[None, :] < live_rows[:, None]
    weights = jnp.where(inside[:, :, None], weights, 0.0).astype(jnp.bfloat16)
    weights32 = weights.astype(jnp.float32)
    child_sum = jnp.einsum('grk,grd->gkd', weights32, members.astype(jnp.float32))
    child_mass = lax.optimization_barrier(jnp.sum(weights32, axis=1))
    return (child_sum, child_mass)

def reference(emb, centroids, block_parent, block_live):
    group_size = 8
    group_count = BLOCKS // group_size
    members = emb.reshape(group_count, group_size, ROWBLK, D)
    parents = block_parent.reshape(group_count, group_size)
    live_counts = block_live.reshape(group_count, group_size)
    current = centroids
    updated = centroids.astype(jnp.float32)
    for sweep_no in range(ITERS):
        kid_table = current.reshape(PARENTS, KIDS, D)

        def accumulate(carried, pieces):
            total_sum, total_mass = carried
            block_rows, block_par, block_len = pieces
            child_sum, child_mass = block_terms(block_rows, kid_table[block_par], block_len)
            return ((total_sum.at[block_par].add(child_sum), total_mass.at[block_par].add(child_mass)), None)
        start_sums = (jnp.zeros((PARENTS, KIDS, D), jnp.float32), jnp.zeros((PARENTS, KIDS), jnp.float32))
        (total_sum, total_mass), unused = lax.scan(accumulate, start_sums, (members, parents, live_counts))
        previous = current.astype(jnp.float32).reshape(PARENTS, KIDS, D)
        updated = (total_sum + PRIOR * previous) / (total_mass[:, :, None] + PRIOR)
        updated = updated.reshape(CENTS, D)
        if sweep_no + 1 < ITERS:
            current = updated.astype(jnp.bfloat16)
    return updated
```

```python
import functools
import math

import jax
import jax.numpy as jnp
from jax import lax
from jax.experimental import pallas as pl
from jax.experimental.pallas import tpu as pltpu
from jax.sharding import Mesh, PartitionSpec as P

D = 768
KIDS = 64
ROWBLK = 128
ITERS = 2
PRIOR = 64
OWNERS = 8
CAP = 4
SLOTS = OWNERS * CAP
PAR_DEV = 16
ROWS_DEV = PAR_DEV * KIDS
WIDE = D + 128
CHIPS = 16
PIECE = ROWS_DEV // CHIPS

SOFTNESS = 0.8
LOGIT_SCALE = 1.0 / (SOFTNESS * math.sqrt(D))

GROUPS = (
    (0, 0, 0, 0, 4),
    (0, 1, 0, 0, 4),
    (1, 0, 1, 0, 4),
    (-1, 0, 3, 0, 4),
    (1, 1, 1, 0, 4),
    (-1, 1, 3, 0, 4),
    (2, 0, 2, 0, 2),
    (-2, 0, 2, 2, 2),
    (2, 1, 2, 0, 2),
    (-2, 1, 2, 2, 2),
)
SENT = GROUPS[1:]
EARLY = 6
TAG_ROWS = 16


def slot_of(kind, other, rank):
    return (kind * 2 + other) * CAP + rank


def dispatch_kernel(pos_ref, par_ref, live_ref, emb_ref, *refs):
    outs, stay_ref = refs[: len(SENT)], refs[len(SENT)]
    held, tiles, src_ref, kid_ref, len_ref, count_ref, read_sem, sems, tag_sems = refs[len(SENT) + 1 :]
    read = pltpu.make_async_copy(emb_ref, held, read_sem)
    read.start()
    z, core = pos_ref[0], pos_ref[1]
    for s in range(SLOTS):
        src_ref[s] = 0
        kid_ref[s] = 0
        len_ref[s] = 0
    for o in range(OWNERS):
        count_ref[o] = 0

    def place(b, carry):
        parent = par_ref[b]
        owner = parent // PAR_DEV
        rank = count_ref[owner]
        count_ref[owner] = rank + 1
        kind = lax.rem(owner - z + 8, 4)
        other = jnp.where(owner // 4 == core, 0, 1)
        slot = slot_of(kind, other, rank)
        src_ref[slot] = b
        kid_ref[slot] = parent - owner * PAR_DEV
        len_ref[slot] = live_ref[b]
        return carry

    lax.fori_loop(0, par_ref.shape[0], place, 0)
    for k in range(CAP):
        stay_ref[0, k] = src_ref[k]
        stay_ref[1, k] = kid_ref[k]
        stay_ref[2, k] = len_ref[k]
    row = lax.broadcasted_iota(jnp.int32, (TAG_ROWS, 128), 0)
    lane = lax.broadcasted_iota(jnp.int32, (TAG_ROWS, 128), 1)
    copies = []
    for i, (_, other, kind, first, size) in enumerate(SENT):
        tile = jnp.zeros((TAG_ROWS, 128), jnp.int32)
        for k in range(size):
            s = slot_of(kind, other, first + k)
            tile = jnp.where(row == k, jnp.where(lane == 0, kid_ref[s], len_ref[s]), tile)
        tiles[i] = tile.astype(jnp.float32).astype(jnp.bfloat16)
    for i, (_, _, _, _, size) in enumerate(SENT):
        copy = pltpu.make_async_copy(
            tiles.at[i], outs[i].at[pl.ds(size * ROWBLK, TAG_ROWS), pl.ds(0, 128)], tag_sems.at[i]
        )
        copy.start()
        copies.append(copy)
    read.wait()
    for i, (_, other, kind, first, size) in enumerate(SENT):
        for k in range(size):
            s = slot_of(kind, other, first + k)
            block = src_ref[s]
            copy = pltpu.make_async_copy(
                held.at[block], outs[i].at[pl.ds(k * ROWBLK, ROWBLK)], sems.at[s]
            )
            copy.start()
            copies.append(copy)
    for copy in copies:
        copy.wait()


def dispatch(pos, parents, lives, blocks):
    smem = pl.BlockSpec(memory_space=pltpu.SMEM)
    hbm = pl.BlockSpec(memory_space=pl.ANY)
    shapes = [jax.ShapeDtypeStruct((g[4] * ROWBLK + TAG_ROWS, D), jnp.bfloat16) for g in SENT]
    return pl.pallas_call(
        dispatch_kernel,
        out_shape=shapes + [jax.ShapeDtypeStruct((3, CAP), jnp.int32)],
        in_specs=[smem, smem, smem, hbm],
        out_specs=[hbm] * len(SENT) + [smem],
        scratch_shapes=[
            pltpu.VMEM(blocks.shape, jnp.bfloat16),
            pltpu.VMEM((len(SENT), TAG_ROWS, 128), jnp.bfloat16),
            pltpu.SMEM((SLOTS,), jnp.int32),
            pltpu.SMEM((SLOTS,), jnp.int32),
            pltpu.SMEM((SLOTS,), jnp.int32),
            pltpu.SMEM((OWNERS,), jnp.int32),
            pltpu.SemaphoreType.DMA,
            pltpu.SemaphoreType.DMA((SLOTS,)),
            pltpu.SemaphoreType.DMA((len(SENT),)),
        ],
        compiler_params=pltpu.CompilerParams(vmem_limit_bytes=16 * 1024 * 1024),
        cost_estimate=pl.CostEstimate(
            flops=0, bytes_accessed=12 * 1024 * 1024, transcendentals=0
        ),
    )(pos, parents, lives, blocks)


def sums_kernel(picked, resumed, packed, *refs):
    refs = list(refs)
    stay_ref = blocks_ref = None
    local = picked[0] == GROUPS[0]
    if local:
        stay_ref, blocks_ref = refs[0], refs[1]
        del refs[:2]
    sent = picked[1:] if local else picked
    groups, table_ref = refs[: len(sent)], refs[len(sent)]
    del refs[: len(sent) + 1]
    if resumed:
        acc_in, mass_in = refs[:2]
        del refs[:2]
    if packed:
        out_ref, acc, mass = refs[:3]
        del refs[:3]
    else:
        acc, mass = refs[:2]
        del refs[:2]
    rows, squares, tiles, kid_ref, len_ref, sems, tag_sems, sum_sems = refs
    batches = rows.shape[0]

    tag_copies = []
    for i, (ref, (_, _, _, _, size)) in enumerate(zip(groups, sent)):
        copy = pltpu.make_async_copy(
            ref.at[pl.ds(size * ROWBLK, TAG_ROWS), pl.ds(0, 128)], tiles.at[i], tag_sems.at[i]
        )
        copy.start()
        tag_copies.append(copy)
    if resumed:
        sum_copies = [
            pltpu.make_async_copy(acc_in, acc, sum_sems.at[0]),
            pltpu.make_async_copy(mass_in, mass, sum_sems.at[1]),
        ]
        for copy in sum_copies:
            copy.start()
    at = 0
    if local:
        for k in range(CAP):
            pltpu.make_async_copy(
                blocks_ref.at[stay_ref[0, k]], rows.at[0, pl.ds(k * ROWBLK, ROWBLK)], sems.at[0]
            ).start()
            kid_ref[k] = stay_ref[1, k]
            len_ref[k] = stay_ref[2, k]
        at = CAP
    for ref, (_, _, _, _, size) in zip(groups, sent):
        pltpu.make_async_copy(
            ref.at[pl.ds(0, size * ROWBLK)],
            rows.at[at // CAP, pl.ds(at % CAP * ROWBLK, size * ROWBLK)],
            sems.at[at // CAP],
        ).start()
        at += size

    if not resumed:
        acc[...] = jnp.zeros_like(acc)
        mass[...] = jnp.zeros_like(mass)

    def square(p, carry):
        at_p = pl.ds(pl.multiple_of(p * KIDS, KIDS), KIDS)
        kids = table_ref[at_p, :].astype(jnp.float32)
        total = jnp.sum(kids * kids, axis=1, keepdims=True)
        squares[at_p, :] = jnp.broadcast_to(total * LOGIT_SCALE, (KIDS, 128))
        return carry

    lax.fori_loop(0, PAR_DEV, square, 0)
    at = CAP if local else 0
    for i, (_, _, _, _, size) in enumerate(sent):
        tag_copies[i].wait()
        tile = tiles[i].astype(jnp.float32).astype(jnp.int32)
        for k in range(size):
            kid_ref[at] = tile[k, 0]
            len_ref[at] = tile[k, 1]
            at += 1
    if resumed:
        for copy in sum_copies:
            copy.wait()
    lane = lax.broadcasted_iota(jnp.int32, (KIDS, ROWBLK), 1)

    def batch_step(batch, carry):
        pltpu.make_async_copy(rows.at[batch], rows.at[batch], sems.at[batch]).wait()
        places, found = [], []
        for k in range(CAP):
            at_p = pl.ds(pl.multiple_of(kid_ref[batch * CAP + k] * KIDS, KIDS), KIDS)
            products = lax.dot_general(
                table_ref[at_p, :],
                rows[batch, k * ROWBLK : (k + 1) * ROWBLK],
                (((1,), (1,)), ((), ())),
                preferred_element_type=jnp.float32,
            )
            logits = products * (2.0 * LOGIT_SCALE) - squares[at_p, :]
            scaled = jnp.exp(logits - jnp.max(logits, axis=0, keepdims=True))
            weights = scaled / jnp.sum(scaled, axis=0, keepdims=True)
            weights = jnp.where(lane < len_ref[batch * CAP + k], weights, 0.0)
            places.append(at_p)
            found.append(weights.astype(jnp.bfloat16))
        for k in range(CAP):
            acc[places[k], :] += jnp.dot(
                found[k],
                rows[batch, k * ROWBLK : (k + 1) * ROWBLK],
                preferred_element_type=jnp.float32,
            )
            mass[places[k], :] += found[k].astype(jnp.float32)
        return carry

    lax.fori_loop(0, batches, batch_step, 0)

    def finish(p, carry):
        at_p = pl.ds(pl.multiple_of(p * KIDS, KIDS), KIDS)
        total = jnp.broadcast_to(jnp.sum(mass[at_p, :], axis=1, keepdims=True), (KIDS, 128))
        high = total.astype(jnp.bfloat16)
        low = (total - high.astype(jnp.float32)).astype(jnp.bfloat16)
        out_ref[at_p, :D] = acc[at_p, :].astype(jnp.bfloat16)
        out_ref[at_p, D:] = jnp.where(lane < 64, high, low)
        return carry

    if packed:
        lax.fori_loop(0, PAR_DEV, finish, 0)


def partial_sums(picked, stay, blocks, groups, table, before=None, packed=True):
    smem = pl.BlockSpec(memory_space=pltpu.SMEM)
    hbm = pl.BlockSpec(memory_space=pl.ANY)
    vmem = pl.BlockSpec(memory_space=pltpu.VMEM)
    slots = sum(g[4] for g in picked)
    sums = [(ROWS_DEV, D), (ROWS_DEV, 128)]
    args, specs = [], []
    if picked[0] == GROUPS[0]:
        args, specs = [stay, blocks], [smem, hbm]
    args = args + list(groups) + [table]
    specs = specs + [hbm] * len(groups) + [vmem]
    if before is not None:
        args = args + list(before)
        specs = specs + [hbm, hbm]
    if packed:
        shapes, outs = jax.ShapeDtypeStruct((ROWS_DEV, WIDE), jnp.bfloat16), vmem
    else:
        shapes, outs = [jax.ShapeDtypeStruct(s, jnp.float32) for s in sums], [vmem, vmem]
    return pl.pallas_call(
        functools.partial(sums_kernel, picked, before is not None, packed),
        out_shape=shapes,
        in_specs=specs,
        out_specs=outs,
        scratch_shapes=([pltpu.VMEM(s, jnp.float32) for s in sums] if packed else [])
        + [
            pltpu.VMEM((slots // CAP, CAP * ROWBLK, D), jnp.bfloat16),
            pltpu.VMEM((ROWS_DEV, 128), jnp.float32),
            pltpu.VMEM((len(groups), TAG_ROWS, 128), jnp.bfloat16),
            pltpu.SMEM((slots,), jnp.int32),
            pltpu.SMEM((slots,), jnp.int32),
            pltpu.SemaphoreType.DMA((slots // CAP,)),
            pltpu.SemaphoreType.DMA((len(groups),)),
            pltpu.SemaphoreType.DMA((2,)),
        ],
        compiler_params=pltpu.CompilerParams(vmem_limit_bytes=40 * 1024 * 1024),
        cost_estimate=pl.CostEstimate(
            flops=slots * 4 * KIDS * ROWBLK * D,
            bytes_accessed=slots * ROWBLK * D * 2 + ROWS_DEV * (WIDE + D) * 2,
            transcendentals=slots * KIDS * ROWBLK,
        ),
    )(*args)


def move(value, shift, other):
    pairs = []
    for c in range(2):
        for z in range(8):
            pairs.append((c * 8 + z, (c ^ other) * 8 + (z + shift) % 8))
    return lax.ppermute(value, ("c", "z"), pairs)


def swap_cores(value):
    return lax.ppermute(value, "c", [(0, 1), (1, 0)])


def split_mass(value):
    high = lax.reduce_precision(value, 8, 7)
    return high.astype(jnp.bfloat16), (value - high).astype(jnp.bfloat16)


def shards(emb, centroids, block_parent, block_live):
    plane = ("y", "x")
    z = lax.axis_index("z").astype(jnp.int32)
    core = lax.axis_index("c").astype(jnp.int32)
    chip = lax.axis_index(plane)
    home = core == z // 4

    rank = lax.axis_index(("y", "x", "c"))
    piece = move(lax.dynamic_slice_in_dim(centroids, rank * 32, 32, 0), 4, 0)

    blocks = emb.reshape(-1, ROWBLK, D)
    *outgoing, stay = dispatch(jnp.stack([z, core]), block_parent, block_live, blocks)
    arrived = [move(value, g[0], g[1]) for value, g in zip(outgoing, SENT)]
    far = lax.all_to_all(
        jnp.broadcast_to(piece[None], (32, 32, D)).reshape(ROWS_DEV, D),
        ("y", "x", "c"), split_axis=0, concat_axis=0, tiled=True,
    )
    current = jnp.where(home, centroids, far)

    early = partial_sums(
        GROUPS[:EARLY], stay, blocks, arrived[: EARLY - 1], current, packed=False
    )
    sums = partial_sums(GROUPS[EARLY:], stay, blocks, arrived[EARLY - 1 :], current, before=early)

    parts = lax.all_to_all(sums, plane, split_axis=0, concat_axis=0, tiled=True)
    mine = jnp.sum(parts.reshape(CHIPS, PIECE, WIDE).astype(jnp.float32), axis=0)
    total = lax.reduce_precision(mine[:, :D], 8, 7)
    high, low = split_mass(mine[:, D : D + 1] + mine[:, D + 64 : D + 65])
    sent = jnp.concatenate(
        [
            total.astype(jnp.bfloat16),
            jnp.broadcast_to(high, (PIECE, 64)),
            jnp.broadcast_to(low, (PIECE, 64)),
        ],
        axis=1,
    )
    got = move(sent, 4, 0).astype(jnp.float32)
    total = total + got[:, :D]
    mass = (high.astype(jnp.float32) + low.astype(jnp.float32)) + (
        got[:, D : D + 1] + got[:, D + 64 : D + 65]
    )
    prior = lax.dynamic_slice_in_dim(current, chip * PIECE, PIECE, 0).astype(jnp.float32)
    updated = ((total + PRIOR * prior) / (mass + PRIOR)).astype(jnp.bfloat16)
    current = lax.all_to_all(
        jnp.broadcast_to(updated[None], (CHIPS, PIECE, D)).reshape(ROWS_DEV, D),
        plane, split_axis=0, concat_axis=0, tiled=True,
    )
    across = swap_cores(current)

    sums = partial_sums(GROUPS, stay, blocks, arrived, current)
    parts = lax.all_to_all(sums, plane, split_axis=0, concat_axis=0, tiled=True)
    mine = jnp.sum(parts.reshape(CHIPS, PIECE, WIDE).astype(jnp.float32), axis=0)
    total = mine[:, :D]
    mass = mine[:, D : D + 1] + mine[:, D + 64 : D + 65]
    high, low = split_mass(mass)
    sent = jnp.concatenate(
        [
            total.astype(jnp.bfloat16),
            jnp.broadcast_to(high, (PIECE, 64)),
            jnp.broadcast_to(low, (PIECE, 64)),
        ],
        axis=1,
    )
    homeward = [(o // 4 * 8 + (o + 4) % 8, o // 4 * 8 + o) for o in range(8)]
    got = lax.ppermute(sent, ("c", "z"), homeward).astype(jnp.float32)
    total = total + got[:, :D]
    mass = mass + (got[:, D : D + 1] + got[:, D + 64 : D + 65])
    prior = lax.dynamic_slice_in_dim(current, chip * PIECE, PIECE, 0).astype(jnp.float32)
    step = ((total - mass * prior) / (mass + PRIOR)).astype(jnp.bfloat16)

    half = PIECE // 2
    step = jnp.where(home, step, swap_cores(step))
    step = jnp.where(core == 0, step[:half], step[half:])
    step = lax.all_to_all(
        jnp.broadcast_to(step[None], (CHIPS, half, D)).reshape(ROWS_DEV // 2, D),
        plane, split_axis=0, concat_axis=0, tiled=True,
    )
    others = swap_cores(step)
    first = jnp.where(core == 0, step, others).reshape(CHIPS, half, D)
    second = jnp.where(core == 0, others, step).reshape(CHIPS, half, D)
    step = jnp.stack([first, second], axis=1).reshape(ROWS_DEV, D)
    return jnp.where(home, current, across).astype(jnp.float32) + step.astype(jnp.float32)


def solution(mesh):
    split = Mesh(mesh.devices.reshape(4, 4, 2, 8), ("y", "x", "c", "z"))
    all_axes = ("y", "x", "c", "z")
    placed = (P(all_axes, None), P("z", None), P(all_axes), P(all_axes))
    return jax.shard_map(
        shards, mesh=split, in_specs=placed, out_specs=P("z", None), check_vma=False
    )
```

```python
import functools
import math

import jax
import jax.numpy as jnp
from jax import lax
from jax.experimental import pallas as pl
from jax.experimental.pallas import tpu as pltpu
from jax.sharding import Mesh, PartitionSpec as P

D = 768
KIDS = 64
ROWBLK = 128
ITERS = 2
PRIOR = 64
OWNERS = 8
CAP = 4
SLOTS = OWNERS * CAP
PAR_DEV = 16
ROWS_DEV = PAR_DEV * KIDS
HALF = ROWS_DEV // 2
CHIPS = 8
PIECE = HALF // CHIPS
WIDE = D + 128

SOFTNESS = 0.8
LOGIT_SCALE = 1.0 / (SOFTNESS * math.sqrt(D))

FAR = 3

GROUPS = (
    (0, 0, 5),
    (1, 0, 5),
    (0, 6, 1),
    (0, 4, 7),
    (1, 6, 1),
    (1, 4, 7),
    (0, 2, 3),
    (1, 2, 3),
)
MOVES = {0: 0, 5: 0, 1: 1, 6: 1, 4: -1, 7: -1, 2: 2, 3: -2}
EARLY = 6
TAG_ROWS = 16
CHUNK = 8
GROUP_ROWS = CAP * ROWBLK
VMEM_ASKED = 56 * 1024 * 1024


def is_home(z, x):
    return z % 2 == x % 2


def offset_of(group, home):
    other, at_home, elsewhere = group
    return at_home if home != bool(other) else elsewhere


def dispatch_kernel(par_hbm, live_hbm, emb_hbm, *refs):
    outs = refs[: len(GROUPS)]
    par_ref, live_ref, held, built, src_ref, kid_ref, len_ref, count_ref, sems, out_sems = refs[
        len(GROUPS) :
    ]
    reads = [
        pltpu.make_async_copy(par_hbm, par_ref, sems.at[0]),
        pltpu.make_async_copy(live_hbm, live_ref, sems.at[1]),
        pltpu.make_async_copy(emb_hbm, held, sems.at[2]),
    ]
    for read in reads:
        read.start()
    z = lax.axis_index("z")
    home = is_home(z, lax.axis_index("xl"))
    for s in range(SLOTS):
        src_ref[s] = 0
        kid_ref[s] = 0
        len_ref[s] = 0
    for o in range(OWNERS):
        count_ref[o] = 0
    reads[0].wait()
    reads[1].wait()
    for b in range(held.shape[0]):
        parent = par_ref[b]
        owner = lax.shift_right_logical(parent, 4)
        rank = count_ref[owner]
        count_ref[owner] = rank + 1
        slot = lax.bitwise_and(owner - z, OWNERS - 1) * CAP + rank
        src_ref[slot] = b
        kid_ref[slot] = lax.bitwise_and(parent, PAR_DEV - 1)
        len_ref[slot] = live_ref[b]
    row = lax.broadcasted_iota(jnp.int32, (TAG_ROWS, 128), 0)
    lane = lax.broadcasted_iota(jnp.int32, (TAG_ROWS, 128), 1)
    firsts = []
    for other, at_home, elsewhere in GROUPS:
        here, there = (elsewhere, at_home) if other else (at_home, elsewhere)
        firsts.append(jnp.where(home, here, there) * CAP)
    for i, first in enumerate(firsts):
        tile = jnp.zeros((TAG_ROWS, 128), jnp.int32)
        for k in range(CAP):
            s = first + k
            tile = jnp.where(row == k, jnp.where(lane == 0, kid_ref[s], len_ref[s]), tile)
        built[i, GROUP_ROWS:, :128] = tile.astype(jnp.float32).astype(jnp.bfloat16)
    reads[2].wait()
    writes = []
    for i, first in enumerate(firsts):
        for k in range(CAP):
            built[i, k * ROWBLK : (k + 1) * ROWBLK, :] = held[src_ref[first + k]]
        write = pltpu.make_async_copy(built.at[i], outs[i], out_sems.at[i])
        write.start()
        writes.append(write)
    for write in writes:
        write.wait()


def dispatch(parents, lives, blocks):
    hbm = pl.BlockSpec(memory_space=pl.ANY)
    shape = jax.ShapeDtypeStruct((GROUP_ROWS + TAG_ROWS, D), jnp.bfloat16)
    return pl.pallas_call(
        dispatch_kernel,
        out_shape=[shape] * len(GROUPS),
        in_specs=[hbm] * 3,
        out_specs=[hbm] * len(GROUPS),
        scratch_shapes=[
            pltpu.SMEM(parents.shape, jnp.int32),
            pltpu.SMEM(lives.shape, jnp.int32),
            pltpu.VMEM(blocks.shape, jnp.bfloat16),
            pltpu.VMEM((len(GROUPS), *shape.shape), jnp.bfloat16),
            pltpu.SMEM((SLOTS,), jnp.int32),
            pltpu.SMEM((SLOTS,), jnp.int32),
            pltpu.SMEM((SLOTS,), jnp.int32),
            pltpu.SMEM((OWNERS,), jnp.int32),
            pltpu.SemaphoreType.DMA((3,)),
            pltpu.SemaphoreType.DMA((len(GROUPS),)),
        ],
        compiler_params=pltpu.CompilerParams(vmem_limit_bytes=VMEM_ASKED),
        cost_estimate=pl.CostEstimate(
            flops=0, bytes_accessed=12 * 1024 * 1024, transcendentals=0
        ),
    )(parents, lives, blocks)


def sums_kernel(count, listed, resumed, packed, *refs):
    refs = list(refs)
    groups = refs[:count]
    tables, tags_in = refs[count : count + 1 + listed], refs[count + 1 + listed : count + 1 + 3 * listed]
    del refs[: count + 1 + 3 * listed]
    if resumed:
        state_in = refs.pop(0)
    if packed:
        keep_ref, send_ref = refs[:2]
        del refs[:2]
    else:
        state_out = refs.pop(0)
    if not listed:
        tags_ref = refs.pop(0)
    state, table, rows, slot_ref, kid_ref, len_ref, sems, state_sem = refs
    tall = GROUP_ROWS + TAG_ROWS
    reads = []
    for i, ref in enumerate(groups):
        read = pltpu.make_async_copy(ref, rows.at[pl.ds(i * tall, tall)], sems.at[i])
        read.start()
        reads.append(read)
    if resumed:
        state_read = pltpu.make_async_copy(state_in, state, state_sem)
        state_read.start()
    core = lax.axis_index("c")
    if listed:
        table[:HALF, :] = tables[0][...]
        table[HALF:, :] = tables[1][...]
    else:
        own = pl.multiple_of(core * HALF, HALF)
        table[:HALF, :] = tables[0][pl.ds(own, HALF), :]
        table[HALF:, :] = tables[0][pl.ds(pl.multiple_of(HALF - own, HALF), HALF), :]

    def square(p, carry):
        at_p = pl.ds(pl.multiple_of(p * KIDS, KIDS), KIDS)
        kids = table[at_p, :].astype(jnp.float32)
        total = jnp.sum(kids * kids, axis=1, keepdims=True)
        state[at_p, WIDE:] = jnp.broadcast_to(total * LOGIT_SCALE, (KIDS, 128))
        return carry

    if not resumed:
        state[:, :WIDE] = jnp.zeros((ROWS_DEV, WIDE), jnp.float32)
        lax.fori_loop(0, PAR_DEV, square, 0)

    used = jnp.int32(0)
    for i in range(count):
        if not listed:
            reads[i].wait()
            tile = rows[i * tall + GROUP_ROWS : (i + 1) * tall, :128].astype(jnp.float32)
            tile = tile.astype(jnp.int32)
        for k in range(CAP):
            at = i * CAP + k
            if listed:
                source, at = (tags_in[0], at) if at < EARLY * CAP else (tags_in[1], at - EARLY * CAP)
                kid, length = source[0, at], source[1, at]
            else:
                kid, length = tile[k, 0], tile[k, 1]
                tags_ref[0, at] = kid
                tags_ref[1, at] = length
            slot_ref[used] = i * tall + k * ROWBLK
            kid_ref[used] = lax.bitwise_xor(kid * KIDS, core * HALF)
            len_ref[used] = length
            used = used + jnp.where(length > 0, 1, 0)
    for k in range(CHUNK):
        slot_ref[used + k] = 0
        kid_ref[used + k] = 0
        len_ref[used + k] = 0
    if listed:
        for read in reads:
            read.wait()
    if resumed:
        state_read.wait()
    lane = lax.broadcasted_iota(jnp.int32, (KIDS, ROWBLK), 1)

    def chunk(j, carry):
        places, blocks, found = [], [], []
        for k in range(CHUNK):
            at = j * CHUNK + k
            at_p = pl.ds(pl.multiple_of(kid_ref[at], KIDS), KIDS)
            at_b = pl.ds(pl.multiple_of(slot_ref[at], 16), ROWBLK)
            products = lax.dot_general(
                table[at_p, :],
                rows[at_b, :],
                (((1,), (1,)), ((), ())),
                preferred_element_type=jnp.float32,
            )
            logits = products * (2.0 * LOGIT_SCALE) - state[at_p, WIDE:]
            scaled = jnp.exp(logits - jnp.max(logits, axis=0, keepdims=True))
            weights = scaled / jnp.sum(scaled, axis=0, keepdims=True)
            weights = jnp.where(lane < len_ref[at], weights, 0.0)
            places.append(at_p)
            blocks.append(at_b)
            found.append(weights.astype(jnp.bfloat16))
        for k in range(CHUNK):
            state[places[k], :D] += jnp.dot(
                found[k], rows[blocks[k], :], preferred_element_type=jnp.float32
            )
            state[places[k], D:WIDE] += found[k].astype(jnp.float32)
        return carry

    lax.fori_loop(0, (used + CHUNK - 1) // CHUNK, chunk, 0)

    part = lax.broadcasted_iota(jnp.int32, (KIDS, 128), 1) // 32 - 2 * core

    def finish(p, carry):
        at_p = pl.ds(pl.multiple_of(p * KIDS, KIDS), KIDS)
        for first, out in ((0, keep_ref), (HALF, send_ref)):
            at_s = pl.ds(pl.multiple_of(first + p * KIDS, KIDS), KIDS)
            total = jnp.sum(state[at_s, D:WIDE], axis=1, keepdims=True)
            total = jnp.broadcast_to(total, (KIDS, 128))
            high = total.astype(jnp.bfloat16).astype(jnp.float32)
            out[at_p, :D] = state[at_s, :D].astype(jnp.bfloat16)
            out[at_p, D:] = jnp.where(
                part == 0, high, jnp.where(part == 1, total - high, 0.0)
            ).astype(jnp.bfloat16)
        return carry

    if packed:
        lax.fori_loop(0, PAR_DEV // 2, finish, 0)
    else:
        state_write = pltpu.make_async_copy(state, state_out, state_sem)
        state_write.start()
        state_write.wait()


def partial_sums(groups, tables, tags=(), state=None, packed=True):
    hbm = pl.BlockSpec(memory_space=pl.ANY)
    vmem = pl.BlockSpec(memory_space=pltpu.VMEM)
    smem = pl.BlockSpec(memory_space=pltpu.SMEM)
    slots = len(groups) * CAP
    shapes = [jax.ShapeDtypeStruct((HALF, WIDE), jnp.bfloat16)] * 2
    specs = [vmem, vmem]
    if not packed:
        shapes, specs = [jax.ShapeDtypeStruct((ROWS_DEV, WIDE + 128), jnp.float32)], [hbm]
    if not tags:
        shapes, specs = shapes + [jax.ShapeDtypeStruct((2, slots), jnp.int32)], specs + [smem]
    states = [] if state is None else [state]
    return pl.pallas_call(
        functools.partial(sums_kernel, len(groups), bool(tags), state is not None, packed),
        out_shape=shapes,
        in_specs=[hbm] * len(groups) + [vmem] * len(tables) + [smem] * len(tags) + [hbm] * len(states),
        out_specs=specs,
        scratch_shapes=[
            pltpu.VMEM((ROWS_DEV, WIDE + 128), jnp.float32),
            pltpu.VMEM((ROWS_DEV, D), jnp.bfloat16),
            pltpu.VMEM((len(groups) * (GROUP_ROWS + TAG_ROWS), D), jnp.bfloat16),
            pltpu.SMEM((slots + CHUNK,), jnp.int32),
            pltpu.SMEM((slots + CHUNK,), jnp.int32),
            pltpu.SMEM((slots + CHUNK,), jnp.int32),
            pltpu.SemaphoreType.DMA((len(groups),)),
            pltpu.SemaphoreType.DMA,
        ],
        compiler_params=pltpu.CompilerParams(vmem_limit_bytes=VMEM_ASKED),
        cost_estimate=pl.CostEstimate(
            flops=slots * 4 * KIDS * ROWBLK * D,
            bytes_accessed=slots * ROWBLK * D * 2 + ROWS_DEV * (WIDE + D) * 2,
            transcendentals=slots * KIDS * ROWBLK,
        ),
    )(*groups, *tables, *tags, *states)


AROUND = ("xh", "xl", "c", "z")


def permute(value, target):
    pairs = []
    for x in range(4):
        for core in range(2):
            for z in range(8):
                goal = target(x, core, z)
                if goal:
                    to_x, to_core, to_z = goal
                    goal = (to_x % 4 * 2 + to_core) * 8 + to_z % 8
                    pairs.append(((x * 2 + core) * 8 + z, goal))
    return lax.ppermute(value, AROUND, pairs)


def move_group(value, group):
    def target(x, core, z):
        step = MOVES[offset_of(group, is_home(z, x))]
        return (x + group[0] * (1 - 2 * core), core, z + step)

    return permute(value, target)


def swap_planes(value):
    return permute(value, lambda x, core, z: (x, core, z + (FAR if is_home(z, x) else -FAR)))


def to_home(value):
    return permute(value, lambda x, core, z: None if is_home(z, x) else (x, core, z - FAR))


def swap_cores(value):
    return lax.ppermute(value, "c", [(0, 1), (1, 0)])


def exchange(value, axes):
    return lax.all_to_all(value, axes, split_axis=0, concat_axis=0, tiled=True)


def spread(value, count, axes):
    wide = jnp.broadcast_to(value[None], (count, *value.shape))
    return exchange(wide.reshape(count * value.shape[0], value.shape[1]), axes)


def mass_of(value):
    return sum(value[:, D + 32 * part : D + 32 * part + 1] for part in range(4))


def reduced(keep, send):
    both = keep.astype(jnp.float32) + swap_cores(send).astype(jnp.float32)
    parts = exchange(both.astype(jnp.bfloat16), ("y", "xh")).reshape(CHIPS, PIECE, WIDE)
    mine = jnp.sum(parts.astype(jnp.float32), axis=0)
    total = lax.reduce_precision(mine[:, :D], 8, 7)
    mass = mass_of(mine)
    high = lax.reduce_precision(mass, 8, 7)
    low = lax.reduce_precision(mass - high, 8, 7)
    lane = lax.broadcasted_iota(jnp.int32, (PIECE, 128), 1) // 32
    split = jnp.where(lane == 0, high, jnp.where(lane == 1, low, 0.0))
    sent = jnp.concatenate([total, split], axis=1).astype(jnp.bfloat16)
    return mine[:, :D], total, mass, high + low, sent


def shards(emb, centroids, block_parent, block_live):
    z = lax.axis_index("z").astype(jnp.int32)
    core = lax.axis_index("c").astype(jnp.int32)
    odd = lax.axis_index("xl").astype(jnp.int32)
    home = is_home(z, odd)
    first_row = core * HALF + lax.axis_index(("y", "xh")) * PIECE

    rank = lax.axis_index(("y", "xh", "xl", "c"))
    piece = lax.ppermute(
        lax.dynamic_slice_in_dim(centroids, rank * 32, 32, 0),
        "z",
        [(p, (p + FAR) % 8) for p in range(8)],
    )
    outgoing = list(dispatch(block_parent, block_live, emb.reshape(-1, ROWBLK, D)))
    piece, outgoing[2] = lax.optimization_barrier((piece, outgoing[2]))
    far = lax.all_gather(piece, ("y", "xh", "xl", "c"), axis=0, tiled=True)
    arrived = [outgoing[0]] + [move_group(v, g) for v, g in zip(outgoing[1:], GROUPS[1:])]
    table = jnp.where(home, centroids, far)

    state, early_tags = partial_sums(arrived[:EARLY], [table], packed=False)
    keep, send, late_tags = partial_sums(arrived[EARLY:], [table], state=state)

    _, total, _, mass, sent = reduced(keep, send)
    got = swap_planes(sent).astype(jnp.float32)
    total, mass = total + got[:, :D], mass + mass_of(got)
    prior = lax.dynamic_slice_in_dim(table, first_row, PIECE, 0).astype(jnp.float32)
    updated = ((total + PRIOR * prior) / (mass + PRIOR)).astype(jnp.bfloat16)
    own = spread(updated, CHIPS, ("y", "xh"))
    tables = [own, swap_cores(own)]

    keep, send = partial_sums(arrived, tables, tags=(early_tags, late_tags))
    total, _, mass, _, sent = reduced(keep, send)
    got = to_home(sent).astype(jnp.float32)
    total, mass = total + got[:, :D], mass + mass_of(got)
    updated = (total + PRIOR * updated.astype(jnp.float32)) / (mass + PRIOR)

    way = (updated - prior).astype(jnp.bfloat16)
    way = jnp.where(home, way, lax.ppermute(way, "xl", [(0, 1), (1, 0)]))
    way = spread(
        jnp.where(odd == 0, way[: PIECE // 2], way[PIECE // 2 :]), 2 * CHIPS, ("y", "xh", "xl")
    )
    others = swap_cores(way)
    way = jnp.concatenate([jnp.where(core == 0, way, others), jnp.where(core == 0, others, way)])
    return centroids.astype(jnp.float32) + way.astype(jnp.float32)


def solution(mesh):
    split = Mesh(mesh.devices.reshape(4, 2, 2, 2, 8), ("y", *AROUND))
    everywhere = ("y", *AROUND)
    placed = (P(everywhere, None), P("z", None), P(everywhere), P(everywhere))
    return jax.shard_map(
        shards, mesh=split, in_specs=placed, out_specs=P("z", None), check_vma=False
    )
```

```python
import functools
import math

import jax
import jax.numpy as jnp
from jax import lax
from jax.experimental import pallas as pl
from jax.experimental.pallas import tpu as pltpu
from jax.sharding import Mesh, PartitionSpec as P

D = 768
KIDS = 64
ROWBLK = 128
ITERS = 2
PRIOR = 64
OWNERS = 8
CAP = 4
SLOTS = OWNERS * CAP
PAR_DEV = 16
ROWS_DEV = PAR_DEV * KIDS
HALF = ROWS_DEV // 2
CHIPS = 8
PIECE = HALF // CHIPS
WIDE = D + 128

SOFTNESS = 0.8
LOGIT_SCALE = 1.0 / (SOFTNESS * math.sqrt(D))

FAR = 3

GROUPS = (
    (0, 0, 5),
    (1, 0, 5),
    (0, 6, 1),
    (0, 4, 7),
    (1, 6, 1),
    (1, 4, 7),
    (0, 2, 3),
    (1, 2, 3),
)
MOVES = {0: 0, 5: 0, 1: 1, 6: 1, 4: -1, 7: -1, 2: 2, 3: -2}
EARLY = 6
TAG_ROWS = 16
CHUNK = 8
GROUP_ROWS = CAP * ROWBLK
VMEM_ASKED = 24 * 1024 * 1024


def is_home(z, x):
    return z % 2 == x % 2


def offset_of(group, home):
    other, at_home, elsewhere = group
    return at_home if home != bool(other) else elsewhere


def dispatch_kernel(par_hbm, live_hbm, emb_hbm, *refs):
    outs = refs[: len(GROUPS)]
    par_ref, live_ref, held, built, src_ref, kid_ref, len_ref, count_ref, sems, out_sems = refs[
        len(GROUPS) :
    ]
    reads = [
        pltpu.make_async_copy(par_hbm, par_ref, sems.at[0]),
        pltpu.make_async_copy(live_hbm, live_ref, sems.at[1]),
        pltpu.make_async_copy(emb_hbm, held, sems.at[2]),
    ]
    for read in reads:
        read.start()
    z = lax.axis_index("z")
    home = is_home(z, lax.axis_index("xl"))
    for s in range(SLOTS):
        src_ref[s] = 0
        kid_ref[s] = 0
        len_ref[s] = 0
    for o in range(OWNERS):
        count_ref[o] = 0
    reads[0].wait()
    reads[1].wait()
    for b in range(held.shape[0]):
        parent = par_ref[b]
        owner = lax.shift_right_logical(parent, 4)
        rank = count_ref[owner]
        count_ref[owner] = rank + 1
        slot = lax.bitwise_and(owner - z, OWNERS - 1) * CAP + rank
        src_ref[slot] = b
        kid_ref[slot] = lax.bitwise_and(parent, PAR_DEV - 1)
        len_ref[slot] = live_ref[b]
    row = lax.broadcasted_iota(jnp.int32, (TAG_ROWS, 128), 0)
    lane = lax.broadcasted_iota(jnp.int32, (TAG_ROWS, 128), 1)
    firsts = []
    for other, at_home, elsewhere in GROUPS:
        here, there = (elsewhere, at_home) if other else (at_home, elsewhere)
        firsts.append(jnp.where(home, here, there) * CAP)
    for i, first in enumerate(firsts):
        tile = jnp.zeros((TAG_ROWS, 128), jnp.int32)
        for k in range(CAP):
            s = first + k
            tile = jnp.where(row == k, jnp.where(lane == 0, kid_ref[s], len_ref[s]), tile)
        built[i, GROUP_ROWS:, :128] = tile.astype(jnp.float32).astype(jnp.bfloat16)
    reads[2].wait()
    writes = []
    for i, first in enumerate(firsts):
        for k in range(CAP):
            built[i, k * ROWBLK : (k + 1) * ROWBLK, :] = held[src_ref[first + k]]
        write = pltpu.make_async_copy(built.at[i], outs[i], out_sems.at[i])
        write.start()
        writes.append(write)
    for write in writes:
        write.wait()


def dispatch(parents, lives, blocks):
    hbm = pl.BlockSpec(memory_space=pl.ANY)
    shape = jax.ShapeDtypeStruct((GROUP_ROWS + TAG_ROWS, D), jnp.bfloat16)
    return pl.pallas_call(
        dispatch_kernel,
        out_shape=[shape] * len(GROUPS),
        in_specs=[hbm] * 3,
        out_specs=[hbm] * len(GROUPS),
        scratch_shapes=[
            pltpu.SMEM(parents.shape, jnp.int32),
            pltpu.SMEM(lives.shape, jnp.int32),
            pltpu.VMEM(blocks.shape, jnp.bfloat16),
            pltpu.VMEM((len(GROUPS), *shape.shape), jnp.bfloat16),
            pltpu.SMEM((SLOTS,), jnp.int32),
            pltpu.SMEM((SLOTS,), jnp.int32),
            pltpu.SMEM((SLOTS,), jnp.int32),
            pltpu.SMEM((OWNERS,), jnp.int32),
            pltpu.SemaphoreType.DMA((3,)),
            pltpu.SemaphoreType.DMA((len(GROUPS),)),
        ],
        compiler_params=pltpu.CompilerParams(vmem_limit_bytes=56 * 1024 * 1024),
        cost_estimate=pl.CostEstimate(
            flops=0, bytes_accessed=12 * 1024 * 1024, transcendentals=0
        ),
    )(parents, lives, blocks)


def sums_kernel(count, listed, resumed, packed, *refs):
    refs = list(refs)
    groups = refs[:count]
    tables, tags_in = refs[count : count + 1 + listed], refs[count + 1 + listed : count + 1 + 3 * listed]
    del refs[: count + 1 + 3 * listed]
    if resumed:
        state_in = refs.pop(0)
    if packed:
        keep_ref, send_ref = refs[:2]
        del refs[:2]
    else:
        state_out = refs.pop(0)
    if not listed:
        tags_ref = refs.pop(0)
    state, table, rows, slot_ref, kid_ref, len_ref, sems, state_sem = refs
    tall = GROUP_ROWS + TAG_ROWS
    reads = []
    for i, ref in enumerate(groups):
        read = pltpu.make_async_copy(ref, rows.at[pl.ds(i * tall, tall)], sems.at[i])
        read.start()
        reads.append(read)
    if resumed:
        state_read = pltpu.make_async_copy(state_in, state, state_sem)
        state_read.start()
    core = lax.axis_index("c")
    if listed:
        table[:HALF, :] = tables[0][...]
        table[HALF:, :] = tables[1][...]
    else:
        own = pl.multiple_of(core * HALF, HALF)
        table[:HALF, :] = tables[0][pl.ds(own, HALF), :]
        table[HALF:, :] = tables[0][pl.ds(pl.multiple_of(HALF - own, HALF), HALF), :]

    def square(p, carry):
        at_p = pl.ds(pl.multiple_of(p * KIDS, KIDS), KIDS)
        kids = table[at_p, :].astype(jnp.float32)
        total = jnp.sum(kids * kids, axis=1, keepdims=True)
        state[at_p, WIDE:] = jnp.broadcast_to(total * LOGIT_SCALE, (KIDS, 128))
        return carry

    if not resumed:
        state[:, :WIDE] = jnp.zeros((ROWS_DEV, WIDE), jnp.float32)
        lax.fori_loop(0, PAR_DEV, square, 0)

    used = jnp.int32(0)
    for i in range(count):
        if not listed:
            reads[i].wait()
            tile = rows[i * tall + GROUP_ROWS : (i + 1) * tall, :128].astype(jnp.float32)
            tile = tile.astype(jnp.int32)
        for k in range(CAP):
            at = i * CAP + k
            if listed:
                source, at = (tags_in[0], at) if at < EARLY * CAP else (tags_in[1], at - EARLY * CAP)
                kid, length = source[0, at], source[1, at]
            else:
                kid, length = tile[k, 0], tile[k, 1]
                tags_ref[0, at] = kid
                tags_ref[1, at] = length
            slot_ref[used] = i * tall + k * ROWBLK
            kid_ref[used] = lax.bitwise_xor(kid * KIDS, core * HALF)
            len_ref[used] = length
            used = used + jnp.where(length > 0, 1, 0)
    for k in range(CHUNK):
        slot_ref[used + k] = 0
        kid_ref[used + k] = 0
        len_ref[used + k] = 0
    if listed:
        for read in reads:
            read.wait()
    if resumed:
        state_read.wait()
    lane = lax.broadcasted_iota(jnp.int32, (KIDS, ROWBLK), 1)

    def chunk(j, carry):
        places, blocks, found = [], [], []
        for k in range(CHUNK):
            at = j * CHUNK + k
            at_p = pl.ds(pl.multiple_of(kid_ref[at], KIDS), KIDS)
            at_b = pl.ds(pl.multiple_of(slot_ref[at], 16), ROWBLK)
            products = lax.dot_general(
                table[at_p, :],
                rows[at_b, :],
                (((1,), (1,)), ((), ())),
                preferred_element_type=jnp.float32,
            )
            logits = products * (2.0 * LOGIT_SCALE) - state[at_p, WIDE:]
            scaled = jnp.exp(logits - jnp.max(logits, axis=0, keepdims=True))
            weights = scaled / jnp.sum(scaled, axis=0, keepdims=True)
            weights = jnp.where(lane < len_ref[at], weights, 0.0)
            places.append(at_p)
            blocks.append(at_b)
            found.append(weights.astype(jnp.bfloat16))
        for k in range(CHUNK):
            state[places[k], :D] += jnp.dot(
                found[k], rows[blocks[k], :], preferred_element_type=jnp.float32
            )
            state[places[k], D:WIDE] += found[k].astype(jnp.float32)
        return carry

    lax.fori_loop(0, (used + CHUNK - 1) // CHUNK, chunk, 0)

    part = lax.broadcasted_iota(jnp.int32, (KIDS, 128), 1) // 32 - 2 * core

    def finish(p, carry):
        at_p = pl.ds(pl.multiple_of(p * KIDS, KIDS), KIDS)
        for first, out in ((0, keep_ref), (HALF, send_ref)):
            at_s = pl.ds(pl.multiple_of(first + p * KIDS, KIDS), KIDS)
            total = jnp.sum(state[at_s, D:WIDE], axis=1, keepdims=True)
            total = jnp.broadcast_to(total, (KIDS, 128))
            high = total.astype(jnp.bfloat16).astype(jnp.float32)
            out[at_p, :D] = state[at_s, :D].astype(jnp.bfloat16)
            out[at_p, D:] = jnp.where(
                part == 0, high, jnp.where(part == 1, total - high, 0.0)
            ).astype(jnp.bfloat16)
        return carry

    if packed:
        lax.fori_loop(0, PAR_DEV // 2, finish, 0)
    else:
        state_write = pltpu.make_async_copy(state, state_out, state_sem)
        state_write.start()
        state_write.wait()


def partial_sums(groups, tables, tags=(), state=None, packed=True):
    hbm = pl.BlockSpec(memory_space=pl.ANY)
    vmem = pl.BlockSpec(memory_space=pltpu.VMEM)
    smem = pl.BlockSpec(memory_space=pltpu.SMEM)
    slots = len(groups) * CAP
    shapes = [jax.ShapeDtypeStruct((HALF, WIDE), jnp.bfloat16)] * 2
    specs = [vmem, vmem]
    if not packed:
        shapes, specs = [jax.ShapeDtypeStruct((ROWS_DEV, WIDE + 128), jnp.float32)], [hbm]
    if not tags:
        shapes, specs = shapes + [jax.ShapeDtypeStruct((2, slots), jnp.int32)], specs + [smem]
    states = [] if state is None else [state]
    return pl.pallas_call(
        functools.partial(sums_kernel, len(groups), bool(tags), state is not None, packed),
        out_shape=shapes,
        in_specs=[hbm] * len(groups) + [vmem] * len(tables) + [smem] * len(tags) + [hbm] * len(states),
        out_specs=specs,
        scratch_shapes=[
            pltpu.VMEM((ROWS_DEV, WIDE + 128), jnp.float32),
            pltpu.VMEM((ROWS_DEV, D), jnp.bfloat16),
            pltpu.VMEM((len(groups) * (GROUP_ROWS + TAG_ROWS), D), jnp.bfloat16),
            pltpu.SMEM((slots + CHUNK,), jnp.int32),
            pltpu.SMEM((slots + CHUNK,), jnp.int32),
            pltpu.SMEM((slots + CHUNK,), jnp.int32),
            pltpu.SemaphoreType.DMA((len(groups),)),
            pltpu.SemaphoreType.DMA,
        ],
        compiler_params=pltpu.CompilerParams(vmem_limit_bytes=VMEM_ASKED),
        cost_estimate=pl.CostEstimate(
            flops=slots * 4 * KIDS * ROWBLK * D,
            bytes_accessed=slots * ROWBLK * D * 2 + ROWS_DEV * (WIDE + D) * 2,
            transcendentals=slots * KIDS * ROWBLK,
        ),
    )(*groups, *tables, *tags, *states)


AROUND = ("xh", "xl", "c", "z")


def permute(value, target):
    pairs = []
    for x in range(4):
        for core in range(2):
            for z in range(8):
                goal = target(x, core, z)
                if goal:
                    to_x, to_core, to_z = goal
                    goal = (to_x % 4 * 2 + to_core) * 8 + to_z % 8
                    pairs.append(((x * 2 + core) * 8 + z, goal))
    return lax.ppermute(value, AROUND, pairs)


def move_group(value, group):
    def target(x, core, z):
        step = MOVES[offset_of(group, is_home(z, x))]
        return (x + group[0] * (1 - 2 * core), core, z + step)

    return permute(value, target)


def swap_planes(value):
    return permute(value, lambda x, core, z: (x, core, z + (FAR if is_home(z, x) else -FAR)))


def to_home(value):
    return permute(value, lambda x, core, z: None if is_home(z, x) else (x, core, z - FAR))


def swap_cores(value):
    return lax.ppermute(value, "c", [(0, 1), (1, 0)])


def exchange(value, axes):
    return lax.all_to_all(value, axes, split_axis=0, concat_axis=0, tiled=True)


def spread(value, count, axes):
    wide = jnp.broadcast_to(value[None], (count, *value.shape))
    return exchange(wide.reshape(count * value.shape[0], value.shape[1]), axes)


def mass_of(value):
    return sum(value[:, D + 32 * part : D + 32 * part + 1] for part in range(4))


def reduced(keep, send):
    both = keep.astype(jnp.float32) + swap_cores(send).astype(jnp.float32)
    parts = exchange(both.astype(jnp.bfloat16), ("y", "xh")).reshape(CHIPS, PIECE, WIDE)
    mine = jnp.sum(parts.astype(jnp.float32), axis=0)
    total = lax.reduce_precision(mine[:, :D], 8, 7)
    mass = mass_of(mine)
    high = lax.reduce_precision(mass, 8, 7)
    low = lax.reduce_precision(mass - high, 8, 7)
    lane = lax.broadcasted_iota(jnp.int32, (PIECE, 128), 1) // 32
    split = jnp.where(lane == 0, high, jnp.where(lane == 1, low, 0.0))
    sent = jnp.concatenate([total, split], axis=1).astype(jnp.bfloat16)
    return mine[:, :D], total, mass, high + low, sent


def shards(emb, centroids, block_parent, block_live):
    z = lax.axis_index("z").astype(jnp.int32)
    core = lax.axis_index("c").astype(jnp.int32)
    odd = lax.axis_index("xl").astype(jnp.int32)
    home = is_home(z, odd)
    first_row = core * HALF + lax.axis_index(("y", "xh")) * PIECE

    rank = lax.axis_index(("y", "xh", "xl", "c"))
    piece = lax.ppermute(
        lax.dynamic_slice_in_dim(centroids, rank * 32, 32, 0),
        "z",
        [(p, (p + FAR) % 8) for p in range(8)],
    )
    outgoing = list(dispatch(block_parent, block_live, emb.reshape(-1, ROWBLK, D)))
    piece, outgoing[2] = lax.optimization_barrier((piece, outgoing[2]))
    far = lax.all_gather(piece, ("y", "xh", "xl", "c"), axis=0, tiled=True)
    arrived = [outgoing[0]] + [move_group(v, g) for v, g in zip(outgoing[1:], GROUPS[1:])]
    table = jnp.where(home, centroids, far)

    state, early_tags = partial_sums(arrived[:EARLY], [table], packed=False)
    keep, send, late_tags = partial_sums(arrived[EARLY:], [table], state=state)

    _, total, _, mass, sent = reduced(keep, send)
    got = swap_planes(sent).astype(jnp.float32)
    total, mass = total + got[:, :D], mass + mass_of(got)
    prior = lax.dynamic_slice_in_dim(table, first_row, PIECE, 0).astype(jnp.float32)
    updated = ((total + PRIOR * prior) / (mass + PRIOR)).astype(jnp.bfloat16)
    own = spread(updated, CHIPS, ("y", "xh"))
    tables = [own, swap_cores(own)]

    keep, send = partial_sums(arrived, tables, tags=(early_tags, late_tags))
    total, _, mass, _, sent = reduced(keep, send)
    got = to_home(sent).astype(jnp.float32)
    total, mass = total + got[:, :D], mass + mass_of(got)
    updated = (total + PRIOR * updated.astype(jnp.float32)) / (mass + PRIOR)

    way = (updated - prior).astype(jnp.bfloat16)
    way = jnp.where(home, way, lax.ppermute(way, "xl", [(0, 1), (1, 0)]))
    way = spread(
        jnp.where(odd == 0, way[: PIECE // 2], way[PIECE // 2 :]), 2 * CHIPS, ("y", "xh", "xl")
    )
    others = swap_cores(way)
    way = jnp.concatenate([jnp.where(core == 0, way, others), jnp.where(core == 0, others, way)])
    return centroids.astype(jnp.float32) + way.astype(jnp.float32)


def solution(mesh):
    split = Mesh(mesh.devices.reshape(4, 2, 2, 2, 8), ("y", *AROUND))
    everywhere = ("y", *AROUND)
    placed = (P(everywhere, None), P("z", None), P(everywhere), P(everywhere))
    return jax.shard_map(
        shards, mesh=split, in_specs=placed, out_specs=P("z", None), check_vma=False
    )
```

```python
import functools
import math

import jax
import jax.numpy as jnp
from jax import lax
from jax.experimental import pallas as pl
from jax.experimental.pallas import tpu as pltpu
from jax.sharding import Mesh, PartitionSpec as P

D = 768
KIDS = 64
ROWBLK = 128
ITERS = 2
PRIOR = 64
OWNERS = 8
CAP = 4
SLOTS = OWNERS * CAP
PAR_DEV = 16
ROWS_DEV = PAR_DEV * KIDS
HALF = ROWS_DEV // 2
CHIPS = 8
PIECE = HALF // CHIPS
WIDE = D + 128

SOFTNESS = 0.8
LOGIT_SCALE = 1.0 / (SOFTNESS * math.sqrt(D))

FAR = 3

GROUPS = (
    (0, 0, 5),
    (1, 0, 5),
    (0, 6, 1),
    (0, 4, 7),
    (1, 6, 1),
    (1, 4, 7),
    (0, 2, 3),
    (1, 2, 3),
)
MOVES = {0: 0, 5: 0, 1: 1, 6: 1, 4: -1, 7: -1, 2: 2, 3: -2}
EARLY = 6
TAG_ROWS = 16
CHUNK = 8
GROUP_ROWS = CAP * ROWBLK
VMEM_ASKED = 24 * 1024 * 1024


def is_home(z, x):
    return z % 2 == x % 2


def offset_of(group, home):
    other, at_home, elsewhere = group
    return at_home if home != bool(other) else elsewhere


def dispatch_kernel(par_hbm, live_hbm, emb_hbm, *refs):
    outs = refs[: len(GROUPS)]
    par_ref, live_ref, held, built, src_ref, kid_ref, len_ref, count_ref, sems, out_sems = refs[
        len(GROUPS) :
    ]
    reads = [
        pltpu.make_async_copy(par_hbm, par_ref, sems.at[0]),
        pltpu.make_async_copy(live_hbm, live_ref, sems.at[1]),
        pltpu.make_async_copy(emb_hbm, held, sems.at[2]),
    ]
    for read in reads:
        read.start()
    z = lax.axis_index("z")
    home = is_home(z, lax.axis_index("xl"))
    for s in range(SLOTS):
        src_ref[s] = 0
        kid_ref[s] = 0
        len_ref[s] = 0
    for o in range(OWNERS):
        count_ref[o] = 0
    reads[0].wait()
    reads[1].wait()
    for b in range(held.shape[0]):
        parent = par_ref[b]
        owner = lax.shift_right_logical(parent, 4)
        rank = count_ref[owner]
        count_ref[owner] = rank + 1
        slot = lax.bitwise_and(owner - z, OWNERS - 1) * CAP + rank
        src_ref[slot] = b
        kid_ref[slot] = lax.bitwise_and(parent, PAR_DEV - 1)
        len_ref[slot] = live_ref[b]
    row = lax.broadcasted_iota(jnp.int32, (TAG_ROWS, 128), 0)
    lane = lax.broadcasted_iota(jnp.int32, (TAG_ROWS, 128), 1)
    firsts = []
    for other, at_home, elsewhere in GROUPS:
        here, there = (elsewhere, at_home) if other else (at_home, elsewhere)
        firsts.append(jnp.where(home, here, there) * CAP)
    for i, first in enumerate(firsts):
        tile = jnp.zeros((TAG_ROWS, 128), jnp.int32)
        for k in range(CAP):
            s = first + k
            tile = jnp.where(row == k, jnp.where(lane == 0, kid_ref[s], len_ref[s]), tile)
        built[i, GROUP_ROWS:, :128] = tile.astype(jnp.float32).astype(jnp.bfloat16)
    reads[2].wait()
    writes = []
    for i, first in enumerate(firsts):
        for k in range(CAP):
            built[i, k * ROWBLK : (k + 1) * ROWBLK, :] = held[src_ref[first + k]]
        write = pltpu.make_async_copy(built.at[i], outs[i], out_sems.at[i])
        write.start()
        writes.append(write)
    for write in writes:
        write.wait()


def dispatch(parents, lives, blocks):
    hbm = pl.BlockSpec(memory_space=pl.ANY)
    shape = jax.ShapeDtypeStruct((GROUP_ROWS + TAG_ROWS, D), jnp.bfloat16)
    return pl.pallas_call(
        dispatch_kernel,
        out_shape=[shape] * len(GROUPS),
        in_specs=[hbm] * 3,
        out_specs=[hbm] * len(GROUPS),
        scratch_shapes=[
            pltpu.SMEM(parents.shape, jnp.int32),
            pltpu.SMEM(lives.shape, jnp.int32),
            pltpu.VMEM(blocks.shape, jnp.bfloat16),
            pltpu.VMEM((len(GROUPS), *shape.shape), jnp.bfloat16),
            pltpu.SMEM((SLOTS,), jnp.int32),
            pltpu.SMEM((SLOTS,), jnp.int32),
            pltpu.SMEM((SLOTS,), jnp.int32),
            pltpu.SMEM((OWNERS,), jnp.int32),
            pltpu.SemaphoreType.DMA((3,)),
            pltpu.SemaphoreType.DMA((len(GROUPS),)),
        ],
        compiler_params=pltpu.CompilerParams(vmem_limit_bytes=56 * 1024 * 1024),
        cost_estimate=pl.CostEstimate(
            flops=0, bytes_accessed=12 * 1024 * 1024, transcendentals=0
        ),
    )(parents, lives, blocks)


def sums_kernel(count, listed, resumed, packed, *refs):
    refs = list(refs)
    groups = refs[:count]
    tables, tags_in = refs[count : count + 1 + listed], refs[count + 1 + listed : count + 1 + 3 * listed]
    del refs[: count + 1 + 3 * listed]
    if resumed:
        state_in = refs.pop(0)
    if packed:
        keep_ref, send_ref = refs[:2]
        del refs[:2]
    else:
        state_out = refs.pop(0)
    if not listed:
        tags_ref = refs.pop(0)
    state, table, rows, slot_ref, kid_ref, len_ref, sems, state_sem = refs
    tall = GROUP_ROWS + TAG_ROWS
    reads = []
    for i, ref in enumerate(groups):
        read = pltpu.make_async_copy(ref, rows.at[pl.ds(i * tall, tall)], sems.at[i])
        read.start()
        reads.append(read)
    if resumed:
        state_read = pltpu.make_async_copy(state_in, state, state_sem)
        state_read.start()
    core = lax.axis_index("c")
    if listed:
        table[:HALF, :] = tables[0][...]
        table[HALF:, :] = tables[1][...]
    else:
        own = pl.multiple_of(core * HALF, HALF)
        table[:HALF, :] = tables[0][pl.ds(own, HALF), :]
        table[HALF:, :] = tables[0][pl.ds(pl.multiple_of(HALF - own, HALF), HALF), :]

    def square(p, carry):
        at_p = pl.ds(pl.multiple_of(p * KIDS, KIDS), KIDS)
        kids = table[at_p, :].astype(jnp.float32)
        total = jnp.sum(kids * kids, axis=1, keepdims=True)
        state[at_p, WIDE:] = jnp.broadcast_to(total * LOGIT_SCALE, (KIDS, 128))
        return carry

    if not resumed:
        state[:, :WIDE] = jnp.zeros((ROWS_DEV, WIDE), jnp.float32)
        lax.fori_loop(0, PAR_DEV, square, 0, unroll=4)

    used = jnp.int32(0)
    for i in range(count):
        if not listed:
            reads[i].wait()
            tile = rows[i * tall + GROUP_ROWS : (i + 1) * tall, :128].astype(jnp.float32)
            tile = tile.astype(jnp.int32)
        for k in range(CAP):
            at = i * CAP + k
            if listed:
                source, at = (tags_in[0], at) if at < EARLY * CAP else (tags_in[1], at - EARLY * CAP)
                kid, length = source[0, at], source[1, at]
            else:
                kid, length = tile[k, 0], tile[k, 1]
                tags_ref[0, at] = kid
                tags_ref[1, at] = length
            slot_ref[used] = i * tall + k * ROWBLK
            kid_ref[used] = lax.bitwise_xor(kid * KIDS, core * HALF)
            len_ref[used] = length
            used = used + jnp.where(length > 0, 1, 0)
    for k in range(CHUNK):
        slot_ref[used + k] = 0
        kid_ref[used + k] = 0
        len_ref[used + k] = 0
    if listed:
        for read in reads:
            read.wait()
    if resumed:
        state_read.wait()
    lane = lax.broadcasted_iota(jnp.int32, (KIDS, ROWBLK), 1)

    def chunk(j, carry):
        places, blocks, found = [], [], []
        for k in range(CHUNK):
            at = j * CHUNK + k
            at_p = pl.ds(pl.multiple_of(kid_ref[at], KIDS), KIDS)
            at_b = pl.ds(pl.multiple_of(slot_ref[at], 16), ROWBLK)
            products = lax.dot_general(
                table[at_p, :],
                rows[at_b, :],
                (((1,), (1,)), ((), ())),
                preferred_element_type=jnp.float32,
            )
            logits = products * (2.0 * LOGIT_SCALE) - state[at_p, WIDE:]
            scaled = jnp.exp(logits - jnp.max(logits, axis=0, keepdims=True))
            weights = scaled / jnp.sum(scaled, axis=0, keepdims=True)
            weights = jnp.where(lane < len_ref[at], weights, 0.0)
            places.append(at_p)
            blocks.append(at_b)
            found.append(weights.astype(jnp.bfloat16))
        for k in range(CHUNK):
            state[places[k], :D] += jnp.dot(
                found[k], rows[blocks[k], :], preferred_element_type=jnp.float32
            )
            state[places[k], D:WIDE] += found[k].astype(jnp.float32)
        return carry

    lax.fori_loop(0, (used + CHUNK - 1) // CHUNK, chunk, 0)

    part = lax.broadcasted_iota(jnp.int32, (KIDS, 128), 1) // 32 - 2 * core

    def finish(p, carry):
        at_p = pl.ds(pl.multiple_of(p * KIDS, KIDS), KIDS)
        for first, out in ((0, keep_ref), (HALF, send_ref)):
            at_s = pl.ds(pl.multiple_of(first + p * KIDS, KIDS), KIDS)
            total = jnp.sum(state[at_s, D:WIDE], axis=1, keepdims=True)
            total = jnp.broadcast_to(total, (KIDS, 128))
            high = total.astype(jnp.bfloat16).astype(jnp.float32)
            out[at_p, :D] = state[at_s, :D].astype(jnp.bfloat16)
            out[at_p, D:] = jnp.where(
                part == 0, high, jnp.where(part == 1, total - high, 0.0)
            ).astype(jnp.bfloat16)
        return carry

    if packed:
        lax.fori_loop(0, PAR_DEV // 2, finish, 0, unroll=2)
    else:
        state_write = pltpu.make_async_copy(state, state_out, state_sem)
        state_write.start()
        state_write.wait()


def partial_sums(groups, tables, tags=(), state=None, packed=True):
    hbm = pl.BlockSpec(memory_space=pl.ANY)
    vmem = pl.BlockSpec(memory_space=pltpu.VMEM)
    smem = pl.BlockSpec(memory_space=pltpu.SMEM)
    slots = len(groups) * CAP
    shapes = [jax.ShapeDtypeStruct((HALF, WIDE), jnp.bfloat16)] * 2
    specs = [vmem, vmem]
    if not packed:
        shapes, specs = [jax.ShapeDtypeStruct((ROWS_DEV, WIDE + 128), jnp.float32)], [hbm]
    if not tags:
        shapes, specs = shapes + [jax.ShapeDtypeStruct((2, slots), jnp.int32)], specs + [smem]
    states = [] if state is None else [state]
    return pl.pallas_call(
        functools.partial(sums_kernel, len(groups), bool(tags), state is not None, packed),
        out_shape=shapes,
        in_specs=[hbm] * len(groups) + [vmem] * len(tables) + [smem] * len(tags) + [hbm] * len(states),
        out_specs=specs,
        scratch_shapes=[
            pltpu.VMEM((ROWS_DEV, WIDE + 128), jnp.float32),
            pltpu.VMEM((ROWS_DEV, D), jnp.bfloat16),
            pltpu.VMEM((len(groups) * (GROUP_ROWS + TAG_ROWS), D), jnp.bfloat16),
            pltpu.SMEM((slots + CHUNK,), jnp.int32),
            pltpu.SMEM((slots + CHUNK,), jnp.int32),
            pltpu.SMEM((slots + CHUNK,), jnp.int32),
            pltpu.SemaphoreType.DMA((len(groups),)),
            pltpu.SemaphoreType.DMA,
        ],
        compiler_params=pltpu.CompilerParams(vmem_limit_bytes=VMEM_ASKED),
        cost_estimate=pl.CostEstimate(
            flops=slots * 4 * KIDS * ROWBLK * D,
            bytes_accessed=slots * ROWBLK * D * 2 + ROWS_DEV * (WIDE + D) * 2,
            transcendentals=slots * KIDS * ROWBLK,
        ),
    )(*groups, *tables, *tags, *states)


AROUND = ("xh", "xl", "c", "z")


def permute(value, target):
    pairs = []
    for x in range(4):
        for core in range(2):
            for z in range(8):
                goal = target(x, core, z)
                if goal:
                    to_x, to_core, to_z = goal
                    goal = (to_x % 4 * 2 + to_core) * 8 + to_z % 8
                    pairs.append(((x * 2 + core) * 8 + z, goal))
    return lax.ppermute(value, AROUND, pairs)


def move_group(value, group):
    def target(x, core, z):
        step = MOVES[offset_of(group, is_home(z, x))]
        return (x + group[0] * (1 - 2 * core), core, z + step)

    return permute(value, target)


def swap_planes(value):
    return permute(value, lambda x, core, z: (x, core, z + (FAR if is_home(z, x) else -FAR)))


def to_home(value):
    return permute(value, lambda x, core, z: None if is_home(z, x) else (x, core, z - FAR))


def swap_cores(value):
    return lax.ppermute(value, "c", [(0, 1), (1, 0)])


def exchange(value, axes):
    return lax.all_to_all(value, axes, split_axis=0, concat_axis=0, tiled=True)


def spread(value, count, axes):
    wide = jnp.broadcast_to(value[None], (count, *value.shape))
    return exchange(wide.reshape(count * value.shape[0], value.shape[1]), axes)


def mass_of(value):
    parts = [value[:, D + 32 * part : D + 32 * part + 1] for part in range(4)]
    return sum(part.astype(jnp.float32) for part in parts)


def reduced(keep, send):
    both = keep.astype(jnp.float32) + swap_cores(send).astype(jnp.float32)
    parts = exchange(both.astype(jnp.bfloat16), ("y", "xh")).reshape(CHIPS, PIECE, WIDE)
    mine = jnp.sum(parts.astype(jnp.float32), axis=0)
    total = lax.reduce_precision(mine[:, :D], 8, 7)
    mass = mass_of(mine)
    high = lax.reduce_precision(mass, 8, 7)
    low = lax.reduce_precision(mass - high, 8, 7)
    column = lax.broadcasted_iota(jnp.int32, (PIECE, WIDE), 1)
    split = jnp.where(column < D + 32, high, jnp.where(column < D + 64, low, 0.0))
    sent = jnp.where(column < D, mine, split).astype(jnp.bfloat16)
    return mine[:, :D], total, mass, high + low, sent


def shards(emb, centroids, block_parent, block_live):
    z = lax.axis_index("z").astype(jnp.int32)
    core = lax.axis_index("c").astype(jnp.int32)
    odd = lax.axis_index("xl").astype(jnp.int32)
    home = is_home(z, odd)
    first_row = core * HALF + lax.axis_index(("y", "xh")) * PIECE

    rank = lax.axis_index(("y", "xh", "xl", "c"))
    piece = lax.ppermute(
        lax.dynamic_slice_in_dim(centroids, rank * 32, 32, 0),
        "z",
        [(p, (p + FAR) % 8) for p in range(8)],
    )
    outgoing = list(dispatch(block_parent, block_live, emb.reshape(-1, ROWBLK, D)))
    piece, outgoing[2] = lax.optimization_barrier((piece, outgoing[2]))
    far = lax.all_gather(piece, ("y", "xh", "xl", "c"), axis=0, tiled=True)
    arrived = [outgoing[0]] + [move_group(v, g) for v, g in zip(outgoing[1:], GROUPS[1:])]
    table = jnp.where(home, centroids, far)

    state, early_tags = partial_sums(arrived[:EARLY], [table], packed=False)
    keep, send, late_tags = partial_sums(arrived[EARLY:], [table], state=state)

    _, total, _, mass, sent = reduced(keep, send)
    got = swap_planes(sent)
    total, mass = total + got[:, :D].astype(jnp.float32), mass + mass_of(got)
    prior = lax.dynamic_slice_in_dim(table, first_row, PIECE, 0).astype(jnp.float32)
    updated = ((total + PRIOR * prior) / (mass + PRIOR)).astype(jnp.bfloat16)
    own = spread(updated, CHIPS, ("y", "xh"))
    tables = [own, swap_cores(own)]

    keep, send = partial_sums(arrived, tables, tags=(early_tags, late_tags))
    total, _, mass, _, sent = reduced(keep, send)
    got = to_home(sent)
    total, mass = total + got[:, :D].astype(jnp.float32), mass + mass_of(got)
    updated = (total + PRIOR * updated.astype(jnp.float32)) / (mass + PRIOR)

    way = (updated - prior).astype(jnp.bfloat16)
    way = jnp.where(home, way, lax.ppermute(way, "xl", [(0, 1), (1, 0)]))
    way = spread(
        jnp.where(odd == 0, way[: PIECE // 2], way[PIECE // 2 :]), 2 * CHIPS, ("y", "xh", "xl")
    )
    others = swap_cores(way)
    way = jnp.concatenate([jnp.where(core == 0, way, others), jnp.where(core == 0, others, way)])
    return centroids.astype(jnp.float32) + way.astype(jnp.float32)


def solution(mesh):
    split = Mesh(mesh.devices.reshape(4, 2, 2, 2, 8), ("y", *AROUND))
    everywhere = ("y", *AROUND)
    placed = (P(everywhere, None), P("z", None), P(everywhere), P(everywhere))
    return jax.shard_map(
        shards, mesh=split, in_specs=placed, out_specs=P("z", None), check_vma=False
    )
```

```python
import functools
import math

import jax
import jax.numpy as jnp
from jax import lax
from jax.experimental import pallas as pl
from jax.experimental.pallas import tpu as pltpu
from jax.sharding import Mesh, PartitionSpec as P

D = 768
KIDS = 64
ROWBLK = 128
ITERS = 2
PRIOR = 64
OWNERS = 8
CAP = 4
SLOTS = OWNERS * CAP
PAR_DEV = 16
ROWS_DEV = PAR_DEV * KIDS
HALF = ROWS_DEV // 2
CHIPS = 8
PIECE = HALF // CHIPS
WIDE = D + 128

SOFTNESS = 0.8
LOGIT_SCALE = 1.0 / (SOFTNESS * math.sqrt(D))

FAR = 3

GROUPS = (
    (0, 0, 5),
    (1, 0, 5),
    (0, 6, 1),
    (0, 4, 7),
    (0, 2, 3),
    (1, 2, 3),
    (1, 6, 1),
    (1, 4, 7),
)
MOVES = {0: 0, 5: 0, 1: 1, 6: 1, 4: -1, 7: -1, 2: 2, 3: -2}
EARLY = 6
TAG_ROWS = 16
CHUNK = 8
GROUP_ROWS = CAP * ROWBLK
VMEM_ASKED = 24 * 1024 * 1024


def is_home(z, x):
    return z % 2 == x % 2


def offset_of(group, home):
    other, at_home, elsewhere = group
    return at_home if home != bool(other) else elsewhere


def dispatch_kernel(par_hbm, live_hbm, emb_hbm, *refs):
    outs = refs[: len(GROUPS)]
    par_ref, live_ref, held, built, src_ref, kid_ref, len_ref, count_ref, sems, out_sems = refs[
        len(GROUPS) :
    ]
    reads = [
        pltpu.make_async_copy(par_hbm, par_ref, sems.at[0]),
        pltpu.make_async_copy(live_hbm, live_ref, sems.at[1]),
        pltpu.make_async_copy(emb_hbm, held, sems.at[2]),
    ]
    for read in reads:
        read.start()
    z = lax.axis_index("z")
    home = is_home(z, lax.axis_index("xl"))
    for s in range(SLOTS):
        src_ref[s] = 0
        kid_ref[s] = 0
        len_ref[s] = 0
    for o in range(OWNERS):
        count_ref[o] = 0
    reads[0].wait()
    reads[1].wait()
    for b in range(held.shape[0]):
        parent = par_ref[b]
        owner = lax.shift_right_logical(parent, 4)
        rank = count_ref[owner]
        count_ref[owner] = rank + 1
        slot = lax.bitwise_and(owner - z, OWNERS - 1) * CAP + rank
        src_ref[slot] = b
        kid_ref[slot] = lax.bitwise_and(parent, PAR_DEV - 1)
        len_ref[slot] = live_ref[b]
    row = lax.broadcasted_iota(jnp.int32, (TAG_ROWS, 128), 0)
    lane = lax.broadcasted_iota(jnp.int32, (TAG_ROWS, 128), 1)
    firsts = []
    for other, at_home, elsewhere in GROUPS:
        here, there = (elsewhere, at_home) if other else (at_home, elsewhere)
        firsts.append(jnp.where(home, here, there) * CAP)
    for i, first in enumerate(firsts):
        tile = jnp.zeros((TAG_ROWS, 128), jnp.int32)
        for k in range(CAP):
            s = first + k
            tile = jnp.where(row == k, jnp.where(lane == 0, kid_ref[s], len_ref[s]), tile)
        built[i, GROUP_ROWS:, :128] = tile.astype(jnp.float32).astype(jnp.bfloat16)
    reads[2].wait()
    writes = []
    for i, first in enumerate(firsts):
        for k in range(CAP):
            built[i, k * ROWBLK : (k + 1) * ROWBLK, :] = held[src_ref[first + k]]
        write = pltpu.make_async_copy(built.at[i], outs[i], out_sems.at[i])
        write.start()
        writes.append(write)
    for write in writes:
        write.wait()


def dispatch(parents, lives, blocks):
    hbm = pl.BlockSpec(memory_space=pl.ANY)
    shape = jax.ShapeDtypeStruct((GROUP_ROWS + TAG_ROWS, D), jnp.bfloat16)
    return pl.pallas_call(
        dispatch_kernel,
        out_shape=[shape] * len(GROUPS),
        in_specs=[hbm] * 3,
        out_specs=[hbm] * len(GROUPS),
        scratch_shapes=[
            pltpu.SMEM(parents.shape, jnp.int32),
            pltpu.SMEM(lives.shape, jnp.int32),
            pltpu.VMEM(blocks.shape, jnp.bfloat16),
            pltpu.VMEM((len(GROUPS), *shape.shape), jnp.bfloat16),
            pltpu.SMEM((SLOTS,), jnp.int32),
            pltpu.SMEM((SLOTS,), jnp.int32),
            pltpu.SMEM((SLOTS,), jnp.int32),
            pltpu.SMEM((OWNERS,), jnp.int32),
            pltpu.SemaphoreType.DMA((3,)),
            pltpu.SemaphoreType.DMA((len(GROUPS),)),
        ],
        compiler_params=pltpu.CompilerParams(vmem_limit_bytes=56 * 1024 * 1024),
        cost_estimate=pl.CostEstimate(
            flops=0, bytes_accessed=12 * 1024 * 1024, transcendentals=0
        ),
    )(parents, lives, blocks)


def sums_kernel(count, listed, resumed, packed, *refs):
    refs = list(refs)
    groups = refs[:count]
    tables, tags_in = refs[count : count + 1 + listed], refs[count + 1 + listed : count + 1 + 3 * listed]
    del refs[: count + 1 + 3 * listed]
    if resumed:
        state_in = refs.pop(0)
    if packed:
        keep_ref, send_ref = refs[:2]
        del refs[:2]
    else:
        state_out = refs.pop(0)
    if not listed:
        tags_ref = refs.pop(0)
    state, table, rows, slot_ref, kid_ref, len_ref, sems, state_sem = refs
    tall = GROUP_ROWS + TAG_ROWS
    reads = []
    for i, ref in enumerate(groups):
        read = pltpu.make_async_copy(ref, rows.at[pl.ds(i * tall, tall)], sems.at[i])
        read.start()
        reads.append(read)
    if resumed:
        state_read = pltpu.make_async_copy(state_in, state, state_sem)
        state_read.start()
    core = lax.axis_index("c")
    if listed:
        table[:HALF, :] = tables[0][...]
        table[HALF:, :] = tables[1][...]
    else:
        own = pl.multiple_of(core * HALF, HALF)
        table[:HALF, :] = tables[0][pl.ds(own, HALF), :]
        table[HALF:, :] = tables[0][pl.ds(pl.multiple_of(HALF - own, HALF), HALF), :]

    def square(p, carry):
        at_p = pl.ds(pl.multiple_of(p * KIDS, KIDS), KIDS)
        kids = table[at_p, :].astype(jnp.float32)
        total = jnp.sum(kids * kids, axis=1, keepdims=True)
        state[at_p, WIDE:] = jnp.broadcast_to(total * LOGIT_SCALE, (KIDS, 128))
        return carry

    if not resumed:
        state[:, :WIDE] = jnp.zeros((ROWS_DEV, WIDE), jnp.float32)
        lax.fori_loop(0, PAR_DEV, square, 0)

    used = jnp.int32(0)
    for i in range(count):
        if not listed:
            reads[i].wait()
            tile = rows[i * tall + GROUP_ROWS : (i + 1) * tall, :128].astype(jnp.float32)
            tile = tile.astype(jnp.int32)
        for k in range(CAP):
            at = i * CAP + k
            if listed:
                source, at = (tags_in[0], at) if at < EARLY * CAP else (tags_in[1], at - EARLY * CAP)
                kid, length = source[0, at], source[1, at]
            else:
                kid, length = tile[k, 0], tile[k, 1]
                tags_ref[0, at] = kid
                tags_ref[1, at] = length
            slot_ref[used] = i * tall + k * ROWBLK
            kid_ref[used] = lax.bitwise_xor(kid * KIDS, core * HALF)
            len_ref[used] = length
            used = used + jnp.where(length > 0, 1, 0)
    for k in range(CHUNK):
        slot_ref[used + k] = 0
        kid_ref[used + k] = 0
        len_ref[used + k] = 0
    if listed:
        for read in reads:
            read.wait()
    if resumed:
        state_read.wait()
    lane = lax.broadcasted_iota(jnp.int32, (KIDS, ROWBLK), 1)

    def chunk(j, carry):
        places, blocks, found = [], [], []
        for k in range(CHUNK):
            at = j * CHUNK + k
            at_p = pl.ds(pl.multiple_of(kid_ref[at], KIDS), KIDS)
            at_b = pl.ds(pl.multiple_of(slot_ref[at], 16), ROWBLK)
            products = lax.dot_general(
                table[at_p, :],
                rows[at_b, :],
                (((1,), (1,)), ((), ())),
                preferred_element_type=jnp.float32,
            )
            logits = products * (2.0 * LOGIT_SCALE) - state[at_p, WIDE:]
            scaled = jnp.exp(logits - jnp.max(logits, axis=0, keepdims=True))
            weights = scaled / jnp.sum(scaled, axis=0, keepdims=True)
            weights = jnp.where(lane < len_ref[at], weights, 0.0)
            places.append(at_p)
            blocks.append(at_b)
            found.append(weights.astype(jnp.bfloat16))
        for k in range(CHUNK):
            state[places[k], :D] += jnp.dot(
                found[k], rows[blocks[k], :], preferred_element_type=jnp.float32
            )
            state[places[k], D:WIDE] += found[k].astype(jnp.float32)
        return carry

    lax.fori_loop(0, (used + CHUNK - 1) // CHUNK, chunk, 0)

    part = lax.broadcasted_iota(jnp.int32, (KIDS, 128), 1) // 32 - 2 * core

    def finish(p, carry):
        at_p = pl.ds(pl.multiple_of(p * KIDS, KIDS), KIDS)
        for first, out in ((0, keep_ref), (HALF, send_ref)):
            at_s = pl.ds(pl.multiple_of(first + p * KIDS, KIDS), KIDS)
            total = jnp.sum(state[at_s, D:WIDE], axis=1, keepdims=True)
            total = jnp.broadcast_to(total, (KIDS, 128))
            high = total.astype(jnp.bfloat16).astype(jnp.float32)
            out[at_p, :D] = state[at_s, :D].astype(jnp.bfloat16)
            out[at_p, D:] = jnp.where(
                part == 0, high, jnp.where(part == 1, total - high, 0.0)
            ).astype(jnp.bfloat16)
        return carry

    if packed:
        lax.fori_loop(0, PAR_DEV // 2, finish, 0)
    else:
        state_write = pltpu.make_async_copy(state, state_out, state_sem)
        state_write.start()
        state_write.wait()


def partial_sums(groups, tables, tags=(), state=None, packed=True):
    hbm = pl.BlockSpec(memory_space=pl.ANY)
    vmem = pl.BlockSpec(memory_space=pltpu.VMEM)
    smem = pl.BlockSpec(memory_space=pltpu.SMEM)
    slots = len(groups) * CAP
    shapes = [jax.ShapeDtypeStruct((HALF, WIDE), jnp.bfloat16)] * 2
    specs = [vmem, vmem]
    if not packed:
        shapes, specs = [jax.ShapeDtypeStruct((ROWS_DEV, WIDE + 128), jnp.float32)], [hbm]
    if not tags:
        shapes, specs = shapes + [jax.ShapeDtypeStruct((2, slots), jnp.int32)], specs + [smem]
    states = [] if state is None else [state]
    return pl.pallas_call(
        functools.partial(sums_kernel, len(groups), bool(tags), state is not None, packed),
        out_shape=shapes,
        in_specs=[hbm] * len(groups) + [vmem] * len(tables) + [smem] * len(tags) + [hbm] * len(states),
        out_specs=specs,
        scratch_shapes=[
            pltpu.VMEM((ROWS_DEV, WIDE + 128), jnp.float32),
            pltpu.VMEM((ROWS_DEV, D), jnp.bfloat16),
            pltpu.VMEM((len(groups) * (GROUP_ROWS + TAG_ROWS), D), jnp.bfloat16),
            pltpu.SMEM((slots + CHUNK,), jnp.int32),
            pltpu.SMEM((slots + CHUNK,), jnp.int32),
            pltpu.SMEM((slots + CHUNK,), jnp.int32),
            pltpu.SemaphoreType.DMA((len(groups),)),
            pltpu.SemaphoreType.DMA,
        ],
        compiler_params=pltpu.CompilerParams(vmem_limit_bytes=VMEM_ASKED),
        cost_estimate=pl.CostEstimate(
            flops=slots * 4 * KIDS * ROWBLK * D,
            bytes_accessed=slots * ROWBLK * D * 2 + ROWS_DEV * (WIDE + D) * 2,
            transcendentals=slots * KIDS * ROWBLK,
        ),
    )(*groups, *tables, *tags, *states)


AROUND = ("xh", "xl", "c", "z")


def permute(value, target):
    pairs = []
    for x in range(4):
        for core in range(2):
            for z in range(8):
                goal = target(x, core, z)
                if goal:
                    to_x, to_core, to_z = goal
                    goal = (to_x % 4 * 2 + to_core) * 8 + to_z % 8
                    pairs.append(((x * 2 + core) * 8 + z, goal))
    return lax.ppermute(value, AROUND, pairs)


def move_group(value, group):
    def target(x, core, z):
        step = MOVES[offset_of(group, is_home(z, x))]
        return (x + group[0] * (1 - 2 * core), core, z + step)

    return permute(value, target)


def swap_planes(value):
    return permute(value, lambda x, core, z: (x, core, z + (FAR if is_home(z, x) else -FAR)))


def to_home(value):
    return permute(value, lambda x, core, z: None if is_home(z, x) else (x, core, z - FAR))


def swap_cores(value):
    return lax.ppermute(value, "c", [(0, 1), (1, 0)])


def exchange(value, axes):
    return lax.all_to_all(value, axes, split_axis=0, concat_axis=0, tiled=True)


def spread(value, count, axes):
    wide = jnp.broadcast_to(value[None], (count, *value.shape))
    return exchange(wide.reshape(count * value.shape[0], value.shape[1]), axes)


def mass_of(value):
    return sum(value[:, D + 32 * part : D + 32 * part + 1] for part in range(4))


def reduced(keep, send):
    both = keep.astype(jnp.float32) + swap_cores(send).astype(jnp.float32)
    parts = exchange(both.astype(jnp.bfloat16), ("y", "xh")).reshape(CHIPS, PIECE, WIDE)
    mine = jnp.sum(parts.astype(jnp.float32), axis=0)
    total = lax.reduce_precision(mine[:, :D], 8, 7)
    mass = mass_of(mine)
    high = lax.reduce_precision(mass, 8, 7)
    low = lax.reduce_precision(mass - high, 8, 7)
    lane = lax.broadcasted_iota(jnp.int32, (PIECE, 128), 1) // 32
    split = jnp.where(lane == 0, high, jnp.where(lane == 1, low, 0.0))
    sent = jnp.concatenate([total, split], axis=1).astype(jnp.bfloat16)
    return mine[:, :D], total, mass, high + low, sent


def shards(emb, centroids, block_parent, block_live):
    z = lax.axis_index("z").astype(jnp.int32)
    core = lax.axis_index("c").astype(jnp.int32)
    odd = lax.axis_index("xl").astype(jnp.int32)
    home = is_home(z, odd)
    first_row = core * HALF + lax.axis_index(("y", "xh")) * PIECE

    rank = lax.axis_index(("y", "xh", "xl", "c"))
    piece = lax.ppermute(
        lax.dynamic_slice_in_dim(centroids, rank * 32, 32, 0),
        "z",
        [(p, (p + FAR) % 8) for p in range(8)],
    )
    outgoing = list(dispatch(block_parent, block_live, emb.reshape(-1, ROWBLK, D)))
    piece, outgoing[2] = lax.optimization_barrier((piece, outgoing[2]))
    far = lax.all_gather(piece, ("y", "xh", "xl", "c"), axis=0, tiled=True)
    arrived = [outgoing[0]] + [move_group(v, g) for v, g in zip(outgoing[1:], GROUPS[1:])]
    table = jnp.where(home, centroids, far)

    state, early_tags = partial_sums(arrived[:EARLY], [table], packed=False)
    keep, send, late_tags = partial_sums(arrived[EARLY:], [table], state=state)

    _, total, _, mass, sent = reduced(keep, send)
    got = swap_planes(sent).astype(jnp.float32)
    total, mass = total + got[:, :D], mass + mass_of(got)
    prior = lax.dynamic_slice_in_dim(table, first_row, PIECE, 0).astype(jnp.float32)
    updated = ((total + PRIOR * prior) / (mass + PRIOR)).astype(jnp.bfloat16)
    own = spread(updated, CHIPS, ("y", "xh"))
    tables = [own, swap_cores(own)]

    keep, send = partial_sums(arrived, tables, tags=(early_tags, late_tags))
    total, _, mass, _, sent = reduced(keep, send)
    got = to_home(sent).astype(jnp.float32)
    total, mass = total + got[:, :D], mass + mass_of(got)
    updated = (total + PRIOR * updated.astype(jnp.float32)) / (mass + PRIOR)

    way = (updated - prior).astype(jnp.bfloat16)
    way = jnp.where(home, way, lax.ppermute(way, "xl", [(0, 1), (1, 0)]))
    way = spread(
        jnp.where(odd == 0, way[: PIECE // 2], way[PIECE // 2 :]), 2 * CHIPS, ("y", "xh", "xl")
    )
    others = swap_cores(way)
    way = jnp.concatenate([jnp.where(core == 0, way, others), jnp.where(core == 0, others, way)])
    return centroids.astype(jnp.float32) + way.astype(jnp.float32)


def solution(mesh):
    split = Mesh(mesh.devices.reshape(4, 2, 2, 2, 8), ("y", *AROUND))
    everywhere = ("y", *AROUND)
    placed = (P(everywhere, None), P("z", None), P(everywhere), P(everywhere))
    return jax.shard_map(
        shards, mesh=split, in_specs=placed, out_specs=P("z", None), check_vma=False
    )
```
